32 devices in a mesh: groups: 2 (over y), feat: 16 (over z, x, core).
Axes of the slice: x: 2, y: 2, z: 4, core: 2. Of those that a mesh axis runs over, the one named last changes fastest.
Arguments:
- node_features: bfloat16 [768, 16384], P('feat', 'groups'), parts along dimension 1, may hold values from -6 to 6
- neighbors_one: int32 [4096, 25], P('groups'), parts along dimension 0, may hold values from 0 to 8191
- weight_self_one: bfloat16 [768, 1024], replicated, may hold values from -0.21875 to 0.21875
- weight_neigh_one: bfloat16 [768, 1024], replicated, may hold values from -0.21875 to 0.21875
- bias_one: bfloat16 [1024], replicated, may hold values from -3 to 3
- weight_self_two: bfloat16 [1024, 1024], replicated, may hold values from -0.1875 to 0.1875
- weight_neigh_two: bfloat16 [1024, 1024], replicated, may hold values from -0.1875 to 0.1875
- send_rows: int32 [16, 16, 4], P('feat', None, 'groups'), parts along dimension 2, may hold values from 0 to 127
- neighbors_two: int32 [2048, 15], P(('groups', 'feat')), parts along dimension 0, may hold values from 0 to 31
- degree_two: int32 [2048], P(('groups', 'feat')), parts along dimension 0, may hold values from 1 to 15
- out_grad: bfloat16 [2048, 1024], P(('groups', 'feat')), parts along dimension 0, may hold values from -0.1875 to 0.1875
Outputs:
- layer_out: bfloat16 [2048, 1024], P(('groups', 'feat')), parts along dimension 0
- grad_self_one: float32 [768, 2048], P('feat', 'groups'), parts along dimension 1
- grad_neigh_one: float32 [768, 2048], P('feat', 'groups'), parts along dimension 1
- grad_self_two: float32 [1024, 2048], P('feat', 'groups'), parts along dimension 1
- grad_neigh_two: float32 [1024, 2048], P('feat', 'groups'), parts along dimension 1
The draws below stay inside these ranges and needn't reach their ends.
There are 2 independent parts, one for each index of `groups`. The reference program is written for one: setup_inputs(seed, part) draws one part's arguments, and reference() takes and returns one part's arrays. A program takes and returns all parts, laid end to end along the dimension named above; an argument that names none is the same for every part. Nothing has to cross between parts.
Inputs may be any that keep to these rules, and one draw needn't show every extreme that they name: `neighbors_one`: sampled neighbors may repeat. send_rows[s, b, c] is one of the 128 layer-one rows owned by block s, provided in slot c to block b; a row may fill several slots. `neighbors_two`: entries at positions k >= degree_two[j] are ignored.
All inputs are finite; a program needn't handle non-finite values.
Results may differ from the reference program's by a relative error of at most 0.0052.
Values may be sent and summed in bfloat16 or wider, within the bound.
A program may use at most 320 MiB of HBM per device.

```python
import jax
import jax.numpy as jnp
from jax import lax

IN_WIDTH = 768
HIDDEN_SIZE = 1024
OWN_ROWS = 128
OWN_SEEDS = 64
FANOUT_ONE = 25
FANOUT_TWO = 15
SLOTS_PEER = 2
TARGETS = 2048
NODES = 8192
SEEDS = 1024
SLOTS = 32
N_FEAT = 16


def set_ends(entries, own_key, least, largest):
    longest = entries.shape.index(max(entries.shape))
    spots = []
    for shift in (0, 1):
        where = [jax.random.randint(jax.random.fold_in(own_key, axis), (), 0, length) for axis, length in enumerate(entries.shape)]
        where[longest] = (where[longest] + shift) % entries.shape[longest]
        spots.append(tuple(where))
    return entries.at[spots[0]].set(least).at[spots[1]].set(largest)


def steps_of(rng, shape, shards, least, high):
    def one(dim, blocks):
        draws = jax.random.uniform(jax.random.fold_in(jax.random.fold_in(rng, 6), dim), (blocks,), jnp.float32, least / len(shards), high / len(shards))
        return jnp.repeat(jnp.exp(draws), shape[dim] // blocks).reshape((-1,) + (1,) * (len(shape) - dim - 1))

    level = one(*shards[0])
    for cut in shards[1:]:
        level = level * one(*cut)
    return level


def centred(own_key, shape, scale, reach, cuts=(), kind=jnp.bfloat16):
    drawn = scale * jax.random.normal(own_key, shape, jnp.float32)
    if cuts:
        drawn = drawn * steps_of(own_key, shape, cuts, -0.22, 0.18)
    return jnp.clip(drawn, -reach, reach).astype(kind)


def setup_inputs(seed: int = 0, part: int = 0) -> dict:
    arg_keys = jax.random.split(jax.random.key(seed), 12)
    part_splits = jax.random.split(jax.random.fold_in(arg_keys[11], part), 12)
    node_features = centred(part_splits[0], (IN_WIDTH, NODES), 1.0, 6.0, ((0, 16),))
    neighbors_one = set_ends(jax.random.randint(part_splits[1], (TARGETS, FANOUT_ONE), 0, NODES), jax.random.fold_in(part_splits[1], 1), 0, NODES - 1).astype(jnp.int32)
    weight_self_one = centred(arg_keys[2], (IN_WIDTH, HIDDEN_SIZE), IN_WIDTH ** -0.5, 0.21875)
    weight_neigh_one = centred(arg_keys[3], (IN_WIDTH, HIDDEN_SIZE), IN_WIDTH ** -0.5, 0.21875)
    bias_one = centred(arg_keys[4], (HIDDEN_SIZE,), 0.5, 3.0)
    weight_self_two = centred(arg_keys[5], (HIDDEN_SIZE, HIDDEN_SIZE), HIDDEN_SIZE ** -0.5, 0.1875)
    weight_neigh_two = centred(arg_keys[6], (HIDDEN_SIZE, HIDDEN_SIZE), HIDDEN_SIZE ** -0.5, 0.1875)
    send_rows = set_ends(jax.random.randint(part_splits[7], (N_FEAT, N_FEAT, SLOTS_PEER), 0, OWN_ROWS), jax.random.fold_in(part_splits[7], 1), 0, OWN_ROWS - 1).astype(jnp.int32)
    neighbors_two = set_ends(jax.random.randint(part_splits[8], (SEEDS, FANOUT_TWO), 0, SLOTS), jax.random.fold_in(part_splits[8], 1), 0, SLOTS - 1).astype(jnp.int32)
    degree_two = set_ends(jax.random.randint(part_splits[9], (SEEDS,), 1, FANOUT_TWO + 1), jax.random.fold_in(part_splits[9], 1), 1, FANOUT_TWO).astype(jnp.int32)
    out_grad = centred(part_splits[10], (SEEDS, HIDDEN_SIZE), (1.0 / SEEDS ** 0.5), 0.1875, ((0, 16),))
    return {"node_features": node_features, "neighbors_one": neighbors_one, "weight_self_one": weight_self_one, "weight_neigh_one": weight_neigh_one, "bias_one": bias_one, "weight_self_two": weight_self_two, "weight_neigh_two": weight_neigh_two, "send_rows": send_rows, "neighbors_two": neighbors_two, "degree_two": degree_two, "out_grad": out_grad}


def gelu_tanh(argument):
    return jax.nn.gelu(argument, approximate=True)

def contract_lead(left_side, right_side):
    return lax.dot_general(left_side, right_side, (((0,), (0,)), ((), ())), preferred_element_type=jnp.float32)

def contract_last(left_side, right_side):
    return lax.dot_general(left_side, right_side, (((1,), (1,)), ((), ())), preferred_element_type=jnp.float32)

def contract_inner(left_side, right_side):
    return lax.dot_general(left_side, right_side, (((1,), (0,)), ((), ())), preferred_element_type=jnp.float32)

def reference(node_features, neighbors_one, weight_self_one, weight_neigh_one, bias_one, weight_self_two, weight_neigh_two, send_rows, neighbors_two, degree_two, out_grad):
    self_feats = node_features[:, :TARGETS]

    def add_neighbor(fan_index, running):
        column = lax.dynamic_slice_in_dim(neighbors_one, fan_index, 1, 1)[:, 0]
        return running + jnp.take(node_features, column, axis=1).astype(jnp.float32)
    summed_one = lax.fori_loop(0, FANOUT_ONE, add_neighbor, jnp.zeros((IN_WIDTH, TARGETS), jnp.float32))
    mean_one = (summed_one / FANOUT_ONE).astype(jnp.bfloat16)
    pre_one = contract_lead(self_feats, weight_self_one) + contract_lead(mean_one, weight_neigh_one) + bias_one.astype(jnp.float32)
    hidden_one = gelu_tanh(pre_one).astype(jnp.bfloat16)
    seed_index = jnp.arange(SEEDS, dtype=jnp.int32)
    seed_block = seed_index // OWN_SEEDS
    seed_rows = seed_block * OWN_ROWS + seed_index % OWN_SEEDS
    source = neighbors_two // SLOTS_PEER
    position = neighbors_two % SLOTS_PEER
    local_row = send_rows[source, seed_block[:, None], position]
    layer_rows = (source * OWN_ROWS + local_row).astype(jnp.int32)
    keep_mask = (jnp.arange(FANOUT_TWO, dtype=jnp.int32)[None, :] < degree_two[:, None]).astype(jnp.float32)
    degree_float = degree_two.astype(jnp.float32)[:, None]
    gathered = jnp.take(hidden_one, layer_rows, axis=0).astype(jnp.float32)
    mean_two = (lax.optimization_barrier(jnp.sum(gathered * keep_mask[:, :, None], axis=1)) / degree_float).astype(jnp.bfloat16)
    seed_hidden = jnp.take(hidden_one, seed_rows, axis=0)
    out_full = jnp.dot(seed_hidden, weight_self_two, preferred_element_type=jnp.float32) + jnp.dot(mean_two, weight_neigh_two, preferred_element_type=jnp.float32)
    layer_out = out_full.astype(jnp.bfloat16)
    grad_self_two = contract_lead(seed_hidden, out_grad)
    grad_neigh_two = contract_lead(mean_two, out_grad)
    back_self = contract_last(out_grad, weight_self_two)
    per_neighbor = contract_last(out_grad, weight_neigh_two) / degree_float
    grad_hidden = jnp.zeros((TARGETS, HIDDEN_SIZE), jnp.float32).at[seed_rows].add(back_self)
    spread = per_neighbor[:, None, :] * keep_mask[:, :, None]
    grad_hidden = grad_hidden.at[layer_rows.reshape(-1)].add(spread.reshape(-1, HIDDEN_SIZE))
    _, pull_back = jax.vjp(gelu_tanh, pre_one)
    grad_pre = pull_back(grad_hidden)[0].astype(jnp.bfloat16)
    grad_self_one = contract_inner(self_feats, grad_pre)
    grad_neigh_one = contract_inner(mean_one, grad_pre)
    return (layer_out, grad_self_one, grad_neigh_one, grad_self_two, grad_neigh_two)
```

```python
import jax
import jax.numpy as jnp
from jax import lax
from jax.experimental import pallas as pl
from jax.experimental.pallas import tpu as pltpu
from jax.sharding import PartitionSpec as P

LANES = 128
UNROLL = 4

def gelu_tanh(argument):
    return jax.nn.gelu(argument, approximate=True)


def contract_lead(left_side, right_side):
    return lax.dot_general(
        left_side, right_side, (((0,), (0,)), ((), ())), preferred_element_type=jnp.float32
    )


def contract_last(left_side, right_side):
    return lax.dot_general(
        left_side, right_side, (((1,), (1,)), ((), ())), preferred_element_type=jnp.float32
    )


def exact_lead(left_side, right_side):
    return lax.dot_general(
        left_side,
        right_side,
        (((0,), (0,)), ((), ())),
        precision=lax.Precision.HIGHEST,
        preferred_element_type=jnp.float32,
    )


def add_rows(ids_ref, table_ref, out_ref):
    fanout = ids_ref.shape[0]

    def body(group, carry):
        for step in range(UNROLL):
            target = group * UNROLL + step
            terms = [table_ref[ids_ref[k, target]] for k in range(fanout)]
            while len(terms) > 1:
                odd = terms[-1:] if len(terms) % 2 else []
                terms = [one + two for one, two in zip(terms[::2], terms[1::2])] + odd
            out_ref[pl.ds(target, 1), :] = terms[0]
        return carry

    lax.fori_loop(0, out_ref.shape[0] // UNROLL, body, 0)


def gather_sum(features, ids):
    width, nodes = features.shape
    fanout, targets = ids.shape
    table = jnp.pad(features.T.astype(jnp.float32), ((0, 0), (0, LANES - width)))
    table = table.reshape(nodes, 1, LANES)
    step_rows = min(512, targets)
    return pl.pallas_call(
        add_rows,
        grid=(targets // step_rows,),
        out_shape=jax.ShapeDtypeStruct((targets, LANES), jnp.float32),
        in_specs=[
            pl.BlockSpec((fanout, step_rows), lambda b: (0, b), memory_space=pltpu.SMEM),
            pl.BlockSpec((nodes, 1, LANES), lambda b: (0, 0, 0), pipeline_mode=pl.Buffered(1)),
        ],
        out_specs=pl.BlockSpec((step_rows, LANES), lambda b: (b, 0)),
        compiler_params=pltpu.CompilerParams(vmem_limit_bytes=nodes * LANES * 4 + (8 << 20)),
        cost_estimate=pl.CostEstimate(
            flops=targets * fanout * LANES,
            bytes_accessed=targets * fanout * LANES * 32,
            transcendentals=0,
        ),
        name="gather_sum",
    )(ids, table)


def shards(
    node_features,
    neighbors_one,
    weight_self_one,
    weight_neigh_one,
    bias_one,
    weight_self_two,
    weight_neigh_two,
    send_rows,
    neighbors_two,
    degree_two,
    out_grad,
):
    devices = lax.axis_size("feat")
    hidden_width = weight_self_two.shape[0]
    own_seeds = out_grad.shape[0]
    targets = neighbors_one.shape[0]
    own_rows = targets // devices
    fanout_one = neighbors_one.shape[1]
    width = node_features.shape[0]
    pairs = devices // 2
    half = pairs * own_rows
    core = lax.axis_index("feat") % 2
    swap = [(d, d ^ 1) for d in range(devices)]
    same_core = [[2 * p + c for p in range(pairs)] for c in range(2)]

    def even_odd(own, other):
        first = jnp.where(core == 0, own, other)
        second = jnp.where(core == 0, other, own)
        return jnp.concatenate([first, second], axis=0)

    def to_blocks(columns):
        return lax.all_to_all(
            columns,
            "feat",
            split_axis=1,
            concat_axis=0,
            axis_index_groups=same_core,
            tiled=True,
        )

    def my_targets(columns):
        cut = columns.reshape(columns.shape[0], pairs, 2, own_rows)
        return lax.dynamic_index_in_dim(cut, core, 2, keepdims=False).reshape(-1, half)

    all_out_grad = lax.all_gather(out_grad, "feat", axis=0, tiled=True)
    partner = lax.ppermute(node_features, "feat", swap)
    self_own = my_targets(node_features[:, :targets])
    self_other = my_targets(partner[:, :targets])
    self_cols = to_blocks(even_odd(self_own, self_other))
    both = jnp.concatenate([node_features, partner], axis=0)
    summed_one = gather_sum(both, my_targets(neighbors_one.T))
    mean_pair = (summed_one[:, : 2 * width] / fanout_one).astype(jnp.bfloat16).T
    mean_own, mean_other = mean_pair[:width], mean_pair[width:]
    mean_cols = to_blocks(even_odd(mean_own, mean_other))
    pre_one = (
        contract_lead(self_cols, weight_self_one)
        + contract_lead(mean_cols, weight_neigh_one)
        + bias_one.astype(jnp.float32)
    )
    hidden_one = gelu_tanh(pre_one).astype(jnp.bfloat16)
    peer_rows = send_rows[0]
    slots_peer = peer_rows.shape[1]
    slot_total = devices * slots_peer
    outgoing = jnp.take(hidden_one, peer_rows.reshape(-1), axis=0).reshape(
        devices, slots_peer, hidden_width
    )
    incoming = lax.all_to_all(outgoing, "feat", split_axis=0, concat_axis=0, tiled=True)
    fanout_two = neighbors_two.shape[1]
    keep_mask = jnp.arange(fanout_two, dtype=jnp.int32)[None, :] < degree_two[:, None]
    slot_ids = jnp.arange(slot_total, dtype=jnp.int32)
    slot_hits = (neighbors_two[:, :, None] == slot_ids[None, None, :]) & keep_mask[:, :, None]
    ref_count = jnp.sum(slot_hits.astype(jnp.float32), axis=1)
    degree_float = degree_two.astype(jnp.float32)[:, None]
    summed_two = jnp.dot(
        ref_count.astype(jnp.bfloat16),
        incoming.reshape(slot_total, hidden_width),
        preferred_element_type=jnp.float32,
    )
    mean_two = (summed_two / degree_float).astype(jnp.bfloat16)
    seed_hidden = hidden_one[:own_seeds]
    out_full = jnp.dot(seed_hidden, weight_self_two, preferred_element_type=jnp.float32) + jnp.dot(
        mean_two, weight_neigh_two, preferred_element_type=jnp.float32
    )
    layer_out = out_full.astype(jnp.bfloat16)
    back_self = contract_last(out_grad, weight_self_two)
    per_neighbor = contract_last(out_grad, weight_neigh_two) / degree_float
    slot_grads = exact_lead(ref_count, per_neighbor)
    returned = lax.all_to_all(
        slot_grads.reshape(devices, slots_peer, hidden_width),
        "feat",
        split_axis=0,
        concat_axis=0,
        tiled=True,
    )
    row_hits = (
        peer_rows.reshape(-1)[:, None] == jnp.arange(own_rows, dtype=jnp.int32)[None, :]
    ).astype(jnp.float32)
    grad_hidden = exact_lead(row_hits, returned.reshape(slot_total, hidden_width))
    grad_hidden = grad_hidden + jnp.pad(back_self, ((0, own_rows - own_seeds), (0, 0)))
    _, pull_back = jax.vjp(gelu_tanh, pre_one)
    grad_pre = pull_back(grad_hidden)[0].astype(jnp.bfloat16)
    same_grad_pre = lax.all_gather(
        grad_pre, "feat", axis=0, axis_index_groups=same_core, tiled=True
    )
    for_other = jnp.dot(
        jnp.concatenate([self_other, mean_other], axis=0),
        same_grad_pre,
        preferred_element_type=jnp.float32,
    )
    from_other = lax.ppermute(for_other, "feat", swap)
    kept = jnp.dot(
        jnp.concatenate([self_own, mean_own], axis=0),
        same_grad_pre,
        preferred_element_type=jnp.float32,
    )
    both_one = kept + from_other
    seed_sides = jnp.stack([seed_hidden, mean_two]).reshape(2, own_seeds, devices, -1)
    seed_sides = lax.all_to_all(
        jnp.transpose(seed_sides, (2, 0, 3, 1)), "feat", split_axis=0, concat_axis=0, tiled=True
    )
    slice_two = seed_sides.shape[2]
    seed_sides = jnp.transpose(seed_sides, (1, 2, 0, 3)).reshape(2 * slice_two, -1)
    both_two = jnp.dot(seed_sides, all_out_grad, preferred_element_type=jnp.float32)
    return (
        layer_out,
        both_one[:width],
        both_one[width:],
        both_two[:slice_two],
        both_two[slice_two:],
    )


def solution(mesh):
    return jax.shard_map(
        shards,
        mesh=mesh,
        in_specs=(
            P("feat", "groups"),
            P("groups", None),
            P(),
            P(),
            P(),
            P(),
            P(),
            P("feat", None, "groups"),
            P(("groups", "feat"), None),
            P(("groups", "feat")),
            P(("groups", "feat"), None),
        ),
        out_specs=(
            P(("groups", "feat"), None),
            P("feat", "groups"),
            P("feat", "groups"),
            P("feat", "groups"),
            P("feat", "groups"),
        ),
        check_vma=False,
    )
```

```python
import jax
import jax.numpy as jnp
from jax import lax
from jax.experimental import pallas as pl
from jax.experimental.pallas import tpu as pltpu
from jax.sharding import PartitionSpec as P

LANES = 128
UNROLL = 4

def gelu_tanh(argument):
    return jax.nn.gelu(argument, approximate=True)


def contract_lead(left_side, right_side):
    return lax.dot_general(
        left_side, right_side, (((0,), (0,)), ((), ())), preferred_element_type=jnp.float32
    )


def contract_last(left_side, right_side):
    return lax.dot_general(
        left_side, right_side, (((1,), (1,)), ((), ())), preferred_element_type=jnp.float32
    )


def exact_lead(left_side, right_side):
    return lax.dot_general(
        left_side,
        right_side,
        (((0,), (0,)), ((), ())),
        precision=lax.Precision.HIGHEST,
        preferred_element_type=jnp.float32,
    )


def add_rows(ids_ref, own_ref, partner_ref, out_ref, table_ref):
    fanout = ids_ref.shape[0]
    width, nodes = own_ref.shape

    @pl.when(pl.program_id(0) == 0)
    def fill_table():
        blank = jnp.zeros((LANES - 2 * width, LANES), jnp.float32)

        def turn(block, carry):
            spot = pl.ds(pl.multiple_of(block * LANES, LANES), LANES)
            own = own_ref[:, spot].astype(jnp.float32)
            partner = partner_ref[:, spot].astype(jnp.float32)
            table_ref[spot, :] = jnp.concatenate([own, partner, blank], axis=0).T
            return carry

        lax.fori_loop(0, nodes // LANES, turn, 0, unroll=4)

    def body(group, carry):
        for step in range(UNROLL):
            target = group * UNROLL + step
            terms = [table_ref[pl.ds(ids_ref[k, target], 1), :] for k in range(fanout)]
            while len(terms) > 1:
                odd = terms[-1:] if len(terms) % 2 else []
                terms = [one + two for one, two in zip(terms[::2], terms[1::2])] + odd
            out_ref[pl.ds(target, 1), :] = terms[0]
        return carry

    lax.fori_loop(0, out_ref.shape[0] // UNROLL, body, 0)


def gather_sum(own, partner, ids):
    width, nodes = own.shape
    fanout, targets = ids.shape
    step_rows = min(512, targets)
    whole = pl.BlockSpec((width, nodes), lambda b: (0, 0), pipeline_mode=pl.Buffered(1))
    return pl.pallas_call(
        add_rows,
        grid=(targets // step_rows,),
        out_shape=jax.ShapeDtypeStruct((targets, LANES), jnp.float32),
        in_specs=[
            pl.BlockSpec((fanout, step_rows), lambda b: (0, b), memory_space=pltpu.SMEM),
            whole,
            whole,
        ],
        out_specs=pl.BlockSpec((step_rows, LANES), lambda b: (b, 0)),
        scratch_shapes=[pltpu.VMEM((nodes, LANES), jnp.float32)],
        compiler_params=pltpu.CompilerParams(
            vmem_limit_bytes=nodes * (LANES + width) * 4 + (8 << 20)
        ),
        cost_estimate=pl.CostEstimate(
            flops=targets * fanout * LANES,
            bytes_accessed=targets * fanout * LANES * 32,
            transcendentals=0,
        ),
        name="gather_sum",
    )(ids, own, partner)


def shards(
    node_features,
    neighbors_one,
    weight_self_one,
    weight_neigh_one,
    bias_one,
    weight_self_two,
    weight_neigh_two,
    send_rows,
    neighbors_two,
    degree_two,
    out_grad,
):
    devices = lax.axis_size("feat")
    hidden_width = weight_self_two.shape[0]
    own_seeds = out_grad.shape[0]
    targets = neighbors_one.shape[0]
    own_rows = targets // devices
    fanout_one = neighbors_one.shape[1]
    width = node_features.shape[0]
    pairs = devices // 2
    half = pairs * own_rows
    core = lax.axis_index("feat") % 2
    swap = [(d, d ^ 1) for d in range(devices)]
    same_core = [[2 * p + c for p in range(pairs)] for c in range(2)]

    def even_odd(own, other):
        first = jnp.where(core == 0, own, other)
        second = jnp.where(core == 0, other, own)
        return jnp.concatenate([first, second], axis=0)

    def to_blocks(columns):
        return lax.all_to_all(
            columns,
            "feat",
            split_axis=1,
            concat_axis=0,
            axis_index_groups=same_core,
            tiled=True,
        )

    def my_targets(columns):
        cut = columns.reshape(columns.shape[0], pairs, 2, own_rows)
        return lax.dynamic_index_in_dim(cut, core, 2, keepdims=False).reshape(-1, half)

    all_out_grad = lax.all_gather(out_grad, "feat", axis=0, tiled=True)
    spare = -width % 16
    features = jnp.pad(node_features, ((0, spare), (0, 0)))
    partner = lax.ppermute(features, "feat", swap)
    self_all = node_features[:, :targets]
    self_cols = lax.all_to_all(self_all, "feat", split_axis=1, concat_axis=0, tiled=True)
    self_own = my_targets(self_all)
    self_other = my_targets(partner[:width, :targets])
    features, self_cols = lax.optimization_barrier((features, self_cols))
    summed_one = gather_sum(features, partner, my_targets(neighbors_one.T))
    mean_pair = (summed_one[:, : 2 * (width + spare)] / fanout_one).astype(jnp.bfloat16).T
    mean_pair, all_out_grad = lax.optimization_barrier((mean_pair, all_out_grad))
    mean_own, mean_other = mean_pair[:width], mean_pair[width + spare :][:width]
    mean_cols = to_blocks(even_odd(mean_own, mean_other))
    pre_one = (
        contract_lead(self_cols, weight_self_one)
        + contract_lead(mean_cols, weight_neigh_one)
        + bias_one.astype(jnp.float32)
    )
    hidden_one = gelu_tanh(pre_one).astype(jnp.bfloat16)
    peer_rows = send_rows[0]
    slots_peer = peer_rows.shape[1]
    slot_total = devices * slots_peer
    row_hits = (
        peer_rows.reshape(-1)[:, None] == jnp.arange(own_rows, dtype=jnp.int32)[None, :]
    ).astype(jnp.float32)
    sent_rows = jnp.dot(
        row_hits.astype(jnp.bfloat16), hidden_one, preferred_element_type=jnp.float32
    ).astype(jnp.bfloat16)
    outgoing = sent_rows.reshape(devices, slots_peer, hidden_width)
    incoming = lax.all_to_all(outgoing, "feat", split_axis=0, concat_axis=0, tiled=True)
    fanout_two = neighbors_two.shape[1]
    keep_mask = jnp.arange(fanout_two, dtype=jnp.int32)[None, :] < degree_two[:, None]
    slot_ids = jnp.arange(slot_total, dtype=jnp.int32)
    slot_hits = (neighbors_two[:, :, None] == slot_ids[None, None, :]) & keep_mask[:, :, None]
    ref_count = jnp.sum(slot_hits.astype(jnp.float32), axis=1)
    degree_float = degree_two.astype(jnp.float32)[:, None]
    slot_out = exact_lead(ref_count / degree_float, out_grad.astype(jnp.float32))
    all_slot_out = lax.all_gather(slot_out.astype(jnp.bfloat16), "feat", axis=0, tiled=True)
    summed_two = jnp.dot(
        ref_count.astype(jnp.bfloat16),
        incoming.reshape(slot_total, hidden_width),
        preferred_element_type=jnp.float32,
    )
    mean_two = (summed_two / degree_float).astype(jnp.bfloat16)
    seed_hidden = hidden_one[:own_seeds]
    out_full = jnp.dot(seed_hidden, weight_self_two, preferred_element_type=jnp.float32) + jnp.dot(
        mean_two, weight_neigh_two, preferred_element_type=jnp.float32
    )
    layer_out = out_full.astype(jnp.bfloat16)
    back_self = contract_last(out_grad, weight_self_two)
    per_neighbor = contract_last(out_grad, weight_neigh_two) / degree_float
    slot_grads = exact_lead(ref_count, per_neighbor)
    returned = lax.all_to_all(
        slot_grads.reshape(devices, slots_peer, hidden_width),
        "feat",
        split_axis=0,
        concat_axis=0,
        tiled=True,
    )
    grad_hidden = exact_lead(row_hits, returned.reshape(slot_total, hidden_width))
    grad_hidden = grad_hidden + jnp.pad(back_self, ((0, own_rows - own_seeds), (0, 0)))
    _, pull_back = jax.vjp(gelu_tanh, pre_one)
    grad_pre = pull_back(grad_hidden)[0].astype(jnp.bfloat16)
    order = list(range(0, pairs, 2)) + list(range(1, pairs, 2))[::-1]
    spots = jnp.asarray(order, jnp.int32)
    mine = jnp.asarray([order.index(p) for p in range(pairs)], jnp.int32)[
        lax.axis_index("feat") // 2
    ]
    onward = [
        (2 * order[i] + c, 2 * order[(i + 1) % pairs] + c) for i in range(pairs) for c in range(2)
    ]
    back = [(there, here) for here, there in onward]
    left = jnp.concatenate([self_other, mean_other, self_own, mean_own], axis=0)
    left = jnp.transpose(left.reshape(4 * width, pairs, own_rows), (1, 0, 2))

    def term(hop, block):
        owner = spots[lax.rem(mine + hop + pairs, pairs)]
        return jnp.dot(
            lax.dynamic_index_in_dim(left, owner, 0, keepdims=False),
            block,
            preferred_element_type=jnp.float32,
        )

    total = term(0, grad_pre)
    going, coming = grad_pre, grad_pre
    for hop in range(1, (pairs + 1) // 2):
        going = lax.ppermute(going, "feat", onward)
        coming = lax.ppermute(coming, "feat", back)
        total = total + term(-hop, going) + term(hop, coming)
    if pairs % 2 == 0:
        cut = own_rows // 2
        first = lax.ppermute(going[:cut], "feat", onward)
        second = lax.ppermute(coming[cut:], "feat", back)
        total = total + term(pairs // 2, jnp.concatenate([first, second], axis=0))
    from_other = lax.ppermute(total[: 2 * width], "feat", swap)
    both_one = total[2 * width :] + from_other

    side_rows = jnp.concatenate([seed_hidden, sent_rows], axis=0)
    side_rows = jnp.transpose(side_rows.reshape(own_seeds + slot_total, devices, -1), (1, 0, 2))
    side_rows = lax.all_to_all(side_rows, "feat", split_axis=0, concat_axis=0, tiled=True)
    slice_two = side_rows.shape[2]
    seed_cols = side_rows[:, :own_seeds].reshape(-1, slice_two)
    sent_cols = side_rows[:, own_seeds:].reshape(devices, devices, slots_peer, slice_two)
    sent_cols = jnp.transpose(sent_cols, (1, 0, 2, 3)).reshape(-1, slice_two)
    return (
        layer_out,
        both_one[:width],
        both_one[width:],
        contract_lead(seed_cols, all_out_grad),
        contract_lead(sent_cols, all_slot_out),
    )


def solution(mesh):
    return jax.shard_map(
        shards,
        mesh=mesh,
        in_specs=(
            P("feat", "groups"),
            P("groups", None),
            P(),
            P(),
            P(),
            P(),
            P(),
            P("feat", None, "groups"),
            P(("groups", "feat"), None),
            P(("groups", "feat")),
            P(("groups", "feat"), None),
        ),
        out_specs=(
            P(("groups", "feat"), None),
            P("feat", "groups"),
            P("feat", "groups"),
            P("feat", "groups"),
            P("feat", "groups"),
        ),
        check_vma=False,
    )
```

```python
import jax
import jax.numpy as jnp
from jax import lax
from jax.experimental import pallas as pl
from jax.experimental.pallas import tpu as pltpu
from jax.sharding import PartitionSpec as P

LANES = 128
UNROLL = 4

def gelu_tanh(argument):
    return jax.nn.gelu(argument, approximate=True)


def contract_lead(left_side, right_side):
    return lax.dot_general(
        left_side, right_side, (((0,), (0,)), ((), ())), preferred_element_type=jnp.float32
    )


def contract_last(left_side, right_side):
    return lax.dot_general(
        left_side, right_side, (((1,), (1,)), ((), ())), preferred_element_type=jnp.float32
    )


def exact_lead(left_side, right_side):
    return lax.dot_general(
        left_side,
        right_side,
        (((0,), (0,)), ((), ())),
        precision=lax.Precision.HIGHEST,
        preferred_element_type=jnp.float32,
    )


def add_rows(ids_ref, own_ref, partner_ref, out_ref, table_ref):
    fanout = ids_ref.shape[0]
    width, nodes = own_ref.shape

    @pl.when(pl.program_id(0) == 0)
    def fill_table():
        blank = jnp.zeros((LANES - 2 * width, LANES), jnp.float32)

        def turn(block, carry):
            spot = pl.ds(pl.multiple_of(block * LANES, LANES), LANES)
            own = own_ref[:, spot].astype(jnp.float32)
            partner = partner_ref[:, spot].astype(jnp.float32)
            table_ref[spot, :] = jnp.concatenate([own, partner, blank], axis=0).T
            return carry

        lax.fori_loop(0, nodes // LANES, turn, 0, unroll=4)

    def body(group, carry):
        for step in range(UNROLL):
            target = group * UNROLL + step
            terms = [table_ref[pl.ds(ids_ref[k, target], 1), :] for k in range(fanout)]
            while len(terms) > 1:
                odd = terms[-1:] if len(terms) % 2 else []
                terms = [one + two for one, two in zip(terms[::2], terms[1::2])] + odd
            out_ref[pl.ds(target, 1), :] = terms[0]
        return carry

    lax.fori_loop(0, out_ref.shape[0] // UNROLL, body, 0)


def gather_sum(own, partner, ids):
    width, nodes = own.shape
    fanout, targets = ids.shape
    step_rows = min(512, targets)
    whole = pl.BlockSpec((width, nodes), lambda b: (0, 0), pipeline_mode=pl.Buffered(1))
    return pl.pallas_call(
        add_rows,
        grid=(targets // step_rows,),
        out_shape=jax.ShapeDtypeStruct((targets, LANES), jnp.float32),
        in_specs=[
            pl.BlockSpec((fanout, step_rows), lambda b: (0, b), memory_space=pltpu.SMEM),
            whole,
            whole,
        ],
        out_specs=pl.BlockSpec((step_rows, LANES), lambda b: (b, 0)),
        scratch_shapes=[pltpu.VMEM((nodes, LANES), jnp.float32)],
        compiler_params=pltpu.CompilerParams(
            vmem_limit_bytes=nodes * (LANES + width) * 4 + (8 << 20)
        ),
        cost_estimate=pl.CostEstimate(
            flops=targets * fanout * LANES,
            bytes_accessed=targets * fanout * LANES * 32,
            transcendentals=0,
        ),
        name="gather_sum",
    )(ids, own, partner)


def shards(
    node_features,
    neighbors_one,
    weight_self_one,
    weight_neigh_one,
    bias_one,
    weight_self_two,
    weight_neigh_two,
    send_rows,
    neighbors_two,
    degree_two,
    out_grad,
):
    devices = lax.axis_size("feat")
    hidden_width = weight_self_two.shape[0]
    own_seeds = out_grad.shape[0]
    targets = neighbors_one.shape[0]
    own_rows = targets // devices
    fanout_one = neighbors_one.shape[1]
    width = node_features.shape[0]
    pairs = devices // 2
    half = pairs * own_rows
    core = lax.axis_index("feat") % 2
    swap = [(d, d ^ 1) for d in range(devices)]
    same_core = [[2 * p + c for p in range(pairs)] for c in range(2)]

    def even_odd(own, other):
        first = jnp.where(core == 0, own, other)
        second = jnp.where(core == 0, other, own)
        return jnp.concatenate([first, second], axis=0)

    def to_blocks(columns):
        return lax.all_to_all(
            columns,
            "feat",
            split_axis=1,
            concat_axis=0,
            axis_index_groups=same_core,
            tiled=True,
        )

    def my_targets(columns):
        cut = columns.reshape(columns.shape[0], pairs, 2, own_rows)
        return lax.dynamic_index_in_dim(cut, core, 2, keepdims=False).reshape(-1, half)

    all_out_grad = lax.all_gather(out_grad, "feat", axis=0, tiled=True)
    spare = -width % 16
    features = jnp.pad(node_features, ((0, spare), (0, 0)))
    partner = lax.ppermute(features, "feat", swap)
    self_all = node_features[:, :targets]
    self_cols = lax.all_to_all(self_all, "feat", split_axis=1, concat_axis=0, tiled=True)
    self_own = my_targets(self_all)
    self_other = my_targets(partner[:width, :targets])
    features, self_cols = lax.optimization_barrier((features, self_cols))
    summed_one = gather_sum(features, partner, my_targets(neighbors_one.T))
    mean_pair = (summed_one[:, : 2 * (width + spare)] / fanout_one).astype(jnp.bfloat16).T
    mean_pair, all_out_grad = lax.optimization_barrier((mean_pair, all_out_grad))
    mean_own, mean_other = mean_pair[:width], mean_pair[width + spare :][:width]
    mean_cols = to_blocks(even_odd(mean_own, mean_other))
    pre_one = (
        contract_lead(self_cols, weight_self_one)
        + contract_lead(mean_cols, weight_neigh_one)
        + bias_one.astype(jnp.float32)
    )
    hidden_one = gelu_tanh(pre_one).astype(jnp.bfloat16)
    peer_rows = send_rows[0]
    slots_peer = peer_rows.shape[1]
    slot_total = devices * slots_peer
    row_hits = (
        peer_rows.reshape(-1)[:, None] == jnp.arange(own_rows, dtype=jnp.int32)[None, :]
    ).astype(jnp.float32)
    sent_rows = jnp.dot(
        row_hits.astype(jnp.bfloat16), hidden_one, preferred_element_type=jnp.float32
    ).astype(jnp.bfloat16)
    outgoing = sent_rows.reshape(devices, slots_peer, hidden_width)
    incoming = lax.all_to_all(outgoing, "feat", split_axis=0, concat_axis=0, tiled=True)
    fanout_two = neighbors_two.shape[1]
    keep_mask = jnp.arange(fanout_two, dtype=jnp.int32)[None, :] < degree_two[:, None]
    slot_ids = jnp.arange(slot_total, dtype=jnp.int32)
    slot_hits = (neighbors_two[:, :, None] == slot_ids[None, None, :]) & keep_mask[:, :, None]
    ref_count = jnp.sum(slot_hits.astype(jnp.float32), axis=1)
    degree_float = degree_two.astype(jnp.float32)[:, None]
    slot_out = exact_lead(ref_count / degree_float, out_grad.astype(jnp.float32))
    all_slot_out = lax.all_gather(slot_out.astype(jnp.bfloat16), "feat", axis=0, tiled=True)
    summed_two = jnp.dot(
        ref_count.astype(jnp.bfloat16),
        incoming.reshape(slot_total, hidden_width),
        preferred_element_type=jnp.float32,
    )
    mean_two = (summed_two / degree_float).astype(jnp.bfloat16)
    seed_hidden = hidden_one[:own_seeds]
    out_full = jnp.dot(seed_hidden, weight_self_two, preferred_element_type=jnp.float32) + jnp.dot(
        mean_two, weight_neigh_two, preferred_element_type=jnp.float32
    )
    layer_out = out_full.astype(jnp.bfloat16)
    back_self = contract_last(out_grad, weight_self_two)
    per_neighbor = contract_last(out_grad, weight_neigh_two) / degree_float
    slot_grads = exact_lead(ref_count, per_neighbor)
    returned = lax.all_to_all(
        slot_grads.reshape(devices, slots_peer, hidden_width),
        "feat",
        split_axis=0,
        concat_axis=0,
        tiled=True,
    )
    grad_hidden = exact_lead(row_hits, returned.reshape(slot_total, hidden_width))
    grad_hidden = grad_hidden + jnp.pad(back_self, ((0, own_rows - own_seeds), (0, 0)))
    _, pull_back = jax.vjp(gelu_tanh, pre_one)
    grad_pre = pull_back(grad_hidden)[0].astype(jnp.bfloat16)
    order = list(range(0, pairs, 2)) + list(range(1, pairs, 2))[::-1]
    evens = (pairs + 1) // 2
    pair = lax.axis_index("feat") // 2
    mine = jnp.where(pair % 2 == 0, pair // 2, pairs - 1 - pair // 2)
    onward = [
        (2 * order[i] + c, 2 * order[(i + 1) % pairs] + c) for i in range(pairs) for c in range(2)
    ]
    back = [(there, here) for here, there in onward]
    left = jnp.concatenate([self_other, mean_other, self_own, mean_own], axis=0)
    left = jnp.transpose(left.reshape(4 * width, pairs, own_rows), (1, 0, 2))

    def term(hop, block):
        spot = lax.rem(mine + hop + pairs, pairs)
        owner = jnp.where(spot < evens, 2 * spot, 2 * (pairs - 1 - spot) + 1)
        return jnp.dot(
            lax.dynamic_index_in_dim(left, owner, 0, keepdims=False),
            block,
            preferred_element_type=jnp.float32,
        )

    side_rows = jnp.concatenate([seed_hidden, sent_rows], axis=0)
    side_rows = jnp.transpose(side_rows.reshape(own_seeds + slot_total, devices, -1), (1, 0, 2))
    total = term(0, grad_pre)
    going, coming = grad_pre, grad_pre
    for hop in range(1, (pairs + 1) // 2):
        going = lax.ppermute(going, "feat", onward)
        coming = lax.ppermute(coming, "feat", back)
        if hop == 1:
            side_rows, going, coming = lax.optimization_barrier((side_rows, going, coming))
        total = total + term(-hop, going) + term(hop, coming)
    if pairs % 2 == 0:
        cut = own_rows // 2
        first = lax.ppermute(going[:cut], "feat", onward)
        second = lax.ppermute(coming[cut:], "feat", back)
        total = total + term(pairs // 2, jnp.concatenate([first, second], axis=0))
    from_other = lax.ppermute(total[: 2 * width], "feat", swap)
    both_one = total[2 * width :] + from_other

    side_rows = lax.all_to_all(side_rows, "feat", split_axis=0, concat_axis=0, tiled=True)
    slice_two = side_rows.shape[2]
    seed_cols = side_rows[:, :own_seeds].reshape(-1, slice_two)
    sent_cols = side_rows[:, own_seeds:].reshape(devices, devices, slots_peer, slice_two)
    sent_cols = jnp.transpose(sent_cols, (1, 0, 2, 3)).reshape(-1, slice_two)
    return (
        layer_out,
        both_one[:width],
        both_one[width:],
        contract_lead(seed_cols, all_out_grad),
        contract_lead(sent_cols, all_slot_out),
    )


def solution(mesh):
    return jax.shard_map(
        shards,
        mesh=mesh,
        in_specs=(
            P("feat", "groups"),
            P("groups", None),
            P(),
            P(),
            P(),
            P(),
            P(),
            P("feat", None, "groups"),
            P(("groups", "feat"), None),
            P(("groups", "feat")),
            P(("groups", "feat"), None),
        ),
        out_specs=(
            P(("groups", "feat"), None),
            P("feat", "groups"),
            P("feat", "groups"),
            P("feat", "groups"),
            P("feat", "groups"),
        ),
        check_vma=False,
    )
```

```python
import jax
import jax.numpy as jnp
from jax import lax
from jax.experimental import pallas as pl
from jax.experimental.pallas import tpu as pltpu
from jax.sharding import PartitionSpec as P

LANES = 128
UNROLL = 4

def gelu_tanh(argument):
    return jax.nn.gelu(argument, approximate=True)


def contract_lead(left_side, right_side):
    return lax.dot_general(
        left_side, right_side, (((0,), (0,)), ((), ())), preferred_element_type=jnp.float32
    )


def contract_last(left_side, right_side):
    return lax.dot_general(
        left_side, right_side, (((1,), (1,)), ((), ())), preferred_element_type=jnp.float32
    )


def exact_lead(left_side, right_side):
    return lax.dot_general(
        left_side,
        right_side,
        (((0,), (0,)), ((), ())),
        precision=lax.Precision.HIGHEST,
        preferred_element_type=jnp.float32,
    )


def add_rows(ids_ref, own_ref, partner_ref, out_ref, table_ref):
    fanout = ids_ref.shape[0]
    width, nodes = own_ref.shape

    @pl.when(pl.program_id(0) == 0)
    def fill_table():
        blank = jnp.zeros((LANES - 2 * width, LANES), jnp.float32)

        def turn(block, carry):
            spot = pl.ds(pl.multiple_of(block * LANES, LANES), LANES)
            own = own_ref[:, spot].astype(jnp.float32)
            partner = partner_ref[:, spot].astype(jnp.float32)
            table_ref[spot, :] = jnp.concatenate([own, partner, blank], axis=0).T
            return carry

        lax.fori_loop(0, nodes // LANES, turn, 0, unroll=4)

    def body(group, carry):
        for step in range(UNROLL):
            target = group * UNROLL + step
            terms = [table_ref[pl.ds(ids_ref[k, target], 1), :] for k in range(fanout)]
            while len(terms) > 1:
                odd = terms[-1:] if len(terms) % 2 else []
                terms = [one + two for one, two in zip(terms[::2], terms[1::2])] + odd
            out_ref[pl.ds(target, 1), :] = terms[0]
        return carry

    lax.fori_loop(0, out_ref.shape[0] // UNROLL, body, 0)


def gather_sum(own, partner, ids):
    width, nodes = own.shape
    fanout, targets = ids.shape
    step_rows = min(512, targets)
    whole = pl.BlockSpec((width, nodes), lambda b: (0, 0), pipeline_mode=pl.Buffered(1))
    return pl.pallas_call(
        add_rows,
        grid=(targets // step_rows,),
        out_shape=jax.ShapeDtypeStruct((targets, LANES), jnp.float32),
        in_specs=[
            pl.BlockSpec((fanout, step_rows), lambda b: (0, b), memory_space=pltpu.SMEM),
            whole,
            whole,
        ],
        out_specs=pl.BlockSpec((step_rows, LANES), lambda b: (b, 0)),
        scratch_shapes=[pltpu.VMEM((nodes, LANES), jnp.float32)],
        compiler_params=pltpu.CompilerParams(
            vmem_limit_bytes=nodes * (LANES + width) * 4 + (8 << 20)
        ),
        cost_estimate=pl.CostEstimate(
            flops=targets * fanout * LANES,
            bytes_accessed=targets * fanout * LANES * 32,
            transcendentals=0,
        ),
        name="gather_sum",
    )(ids, own, partner)


def shards(
    node_features,
    neighbors_one,
    weight_self_one,
    weight_neigh_one,
    bias_one,
    weight_self_two,
    weight_neigh_two,
    send_rows,
    neighbors_two,
    degree_two,
    out_grad,
):
    devices = lax.axis_size("feat")
    hidden_width = weight_self_two.shape[0]
    own_seeds = out_grad.shape[0]
    targets = neighbors_one.shape[0]
    own_rows = targets // devices
    fanout_one = neighbors_one.shape[1]
    width = node_features.shape[0]
    pairs = devices // 2
    half = pairs * own_rows
    core = lax.axis_index("feat") % 2
    swap = [(d, d ^ 1) for d in range(devices)]
    same_core = [[2 * p + c for p in range(pairs)] for c in range(2)]

    def even_odd(own, other):
        first = jnp.where(core == 0, own, other)
        second = jnp.where(core == 0, other, own)
        return jnp.concatenate([first, second], axis=0)

    def to_blocks(columns):
        return lax.all_to_all(
            columns,
            "feat",
            split_axis=1,
            concat_axis=0,
            axis_index_groups=same_core,
            tiled=True,
        )

    def my_targets(columns):
        cut = columns.reshape(columns.shape[0], pairs, 2, own_rows)
        return lax.dynamic_index_in_dim(cut, core, 2, keepdims=False).reshape(-1, half)

    all_out_grad = lax.all_gather(out_grad, "feat", axis=0, tiled=True)
    spare = -width % 16
    features = jnp.pad(node_features, ((0, spare), (0, 0)))
    partner = lax.ppermute(features, "feat", swap)
    self_all = node_features[:, :targets]
    peer_rows = send_rows[0]
    slots_peer = peer_rows.shape[1]
    slot_total = devices * slots_peer
    fanout_two = neighbors_two.shape[1]
    keep_mask = jnp.arange(fanout_two, dtype=jnp.int32)[None, :] < degree_two[:, None]
    slot_ids = jnp.arange(slot_total, dtype=jnp.int32)
    slot_hits = (neighbors_two[:, :, None] == slot_ids[None, None, :]) & keep_mask[:, :, None]
    ref_count = jnp.sum(slot_hits.astype(jnp.float32), axis=1)
    degree_float = degree_two.astype(jnp.float32)[:, None]
    back_self = contract_last(out_grad, weight_self_two)
    per_neighbor = contract_last(out_grad, weight_neigh_two) / degree_float
    slot_grads = exact_lead(ref_count, per_neighbor)
    blocks = jnp.transpose(self_all.reshape(width, devices, own_rows), (1, 0, 2))
    slot_grads = slot_grads.astype(jnp.bfloat16).reshape(devices, -1, own_rows)
    swapped = lax.all_to_all(
        jnp.concatenate([blocks, slot_grads], axis=1),
        "feat",
        split_axis=0,
        concat_axis=0,
        tiled=True,
    )
    self_own = my_targets(self_all)
    self_other = my_targets(partner[:width, :targets])
    features, swapped = lax.optimization_barrier((features, swapped))
    self_cols = swapped[:, :width].reshape(devices * width, own_rows)
    returned = swapped[:, width:].reshape(slot_total, hidden_width)
    summed_one = gather_sum(features, partner, my_targets(neighbors_one.T))
    mean_pair = (summed_one[:, : 2 * (width + spare)] / fanout_one).astype(jnp.bfloat16).T
    mean_pair, all_out_grad = lax.optimization_barrier((mean_pair, all_out_grad))
    mean_own, mean_other = mean_pair[:width], mean_pair[width + spare :][:width]
    mean_cols = to_blocks(even_odd(mean_own, mean_other))
    pre_one = (
        contract_lead(self_cols, weight_self_one)
        + contract_lead(mean_cols, weight_neigh_one)
        + bias_one.astype(jnp.float32)
    )
    hidden_one = gelu_tanh(pre_one).astype(jnp.bfloat16)
    row_hits = (
        peer_rows.reshape(-1)[:, None] == jnp.arange(own_rows, dtype=jnp.int32)[None, :]
    ).astype(jnp.bfloat16)
    sent_rows = jnp.dot(row_hits, hidden_one, preferred_element_type=jnp.float32).astype(
        jnp.bfloat16
    )
    outgoing = sent_rows.reshape(devices, slots_peer, hidden_width)
    slot_out = exact_lead(ref_count / degree_float, out_grad.astype(jnp.float32))
    all_slot_out = lax.all_gather(slot_out.astype(jnp.bfloat16), "feat", axis=0, tiled=True)
    seed_hidden = hidden_one[:own_seeds]
    grad_hidden = contract_lead(row_hits, returned)
    grad_hidden = grad_hidden + jnp.pad(back_self, ((0, own_rows - own_seeds), (0, 0)))
    _, pull_back = jax.vjp(gelu_tanh, pre_one)
    grad_pre = pull_back(grad_hidden)[0].astype(jnp.bfloat16)
    order = list(range(0, pairs, 2)) + list(range(1, pairs, 2))[::-1]
    evens = (pairs + 1) // 2
    pair = lax.axis_index("feat") // 2
    mine = jnp.where(pair % 2 == 0, pair // 2, pairs - 1 - pair // 2)
    onward = [
        (2 * order[i] + c, 2 * order[(i + 1) % pairs] + c) for i in range(pairs) for c in range(2)
    ]
    back = [(there, here) for here, there in onward]
    left = jnp.concatenate([self_other, mean_other, self_own, mean_own], axis=0)
    left = jnp.transpose(left.reshape(4 * width, pairs, own_rows), (1, 0, 2))

    def term(hop, block):
        spot = lax.rem(mine + hop + pairs, pairs)
        owner = jnp.where(spot < evens, 2 * spot, 2 * (pairs - 1 - spot) + 1)
        return jnp.dot(
            lax.dynamic_index_in_dim(left, owner, 0, keepdims=False),
            block,
            preferred_element_type=jnp.float32,
        )

    side_rows = jnp.concatenate([seed_hidden, sent_rows], axis=0)
    side_rows = jnp.transpose(side_rows.reshape(own_seeds + slot_total, devices, -1), (1, 0, 2))
    total = term(0, grad_pre)
    going, coming = grad_pre, grad_pre
    for hop in range(1, (pairs + 1) // 2):
        going = lax.ppermute(going, "feat", onward)
        coming = lax.ppermute(coming, "feat", back)
        if hop == 1:
            outgoing, going, coming = lax.optimization_barrier((outgoing, going, coming))
        if hop == 2:
            side_rows, going, coming = lax.optimization_barrier((side_rows, going, coming))
        total = total + term(-hop, going) + term(hop, coming)
    if pairs % 2 == 0:
        cut = own_rows // 2
        first = lax.ppermute(going[:cut], "feat", onward)
        second = lax.ppermute(coming[cut:], "feat", back)
        total = total + term(pairs // 2, jnp.concatenate([first, second], axis=0))
    from_other = lax.ppermute(total[: 2 * width], "feat", swap)
    both_one = total[2 * width :] + from_other

    incoming = lax.all_to_all(outgoing, "feat", split_axis=0, concat_axis=0, tiled=True)
    summed_two = jnp.dot(
        ref_count.astype(jnp.bfloat16),
        incoming.reshape(slot_total, hidden_width),
        preferred_element_type=jnp.float32,
    )
    mean_two = (summed_two / degree_float).astype(jnp.bfloat16)
    out_full = jnp.dot(seed_hidden, weight_self_two, preferred_element_type=jnp.float32) + jnp.dot(
        mean_two, weight_neigh_two, preferred_element_type=jnp.float32
    )
    layer_out = out_full.astype(jnp.bfloat16)

    side_rows = lax.all_to_all(side_rows, "feat", split_axis=0, concat_axis=0, tiled=True)
    slice_two = side_rows.shape[2]
    seed_cols = side_rows[:, :own_seeds].reshape(-1, slice_two)
    sent_cols = side_rows[:, own_seeds:].reshape(devices, devices, slots_peer, slice_two)
    sent_cols = jnp.transpose(sent_cols, (1, 0, 2, 3)).reshape(-1, slice_two)
    return (
        layer_out,
        both_one[:width],
        both_one[width:],
        contract_lead(seed_cols, all_out_grad),
        contract_lead(sent_cols, all_slot_out),
    )


def solution(mesh):
    return jax.shard_map(
        shards,
        mesh=mesh,
        in_specs=(
            P("feat", "groups"),
            P("groups", None),
            P(),
            P(),
            P(),
            P(),
            P(),
            P("feat", None, "groups"),
            P(("groups", "feat"), None),
            P(("groups", "feat")),
            P(("groups", "feat"), None),
        ),
        out_specs=(
            P(("groups", "feat"), None),
            P("feat", "groups"),
            P("feat", "groups"),
            P("feat", "groups"),
            P("feat", "groups"),
        ),
        check_vma=False,
    )
```

```python
import jax
import jax.numpy as jnp
from jax import lax
from jax.experimental import pallas as pl
from jax.experimental.pallas import tpu as pltpu
from jax.sharding import PartitionSpec as P

LANES = 128
UNROLL = 4

def gelu_tanh(argument):
    return jax.nn.gelu(argument, approximate=True)


def contract_lead(left_side, right_side):
    return lax.dot_general(
        left_side, right_side, (((0,), (0,)), ((), ())), preferred_element_type=jnp.float32
    )


def contract_last(left_side, right_side):
    return lax.dot_general(
        left_side, right_side, (((1,), (1,)), ((), ())), preferred_element_type=jnp.float32
    )


def exact_lead(left_side, right_side):
    return lax.dot_general(
        left_side,
        right_side,
        (((0,), (0,)), ((), ())),
        precision=lax.Precision.HIGHEST,
        preferred_element_type=jnp.float32,
    )


def add_rows(ids_ref, own_ref, partner_ref, out_ref, table_ref):
    fanout = ids_ref.shape[0]
    width, nodes = own_ref.shape

    @pl.when(pl.program_id(0) == 0)
    def fill_table():
        blank = jnp.zeros((LANES - 2 * width, LANES), jnp.float32)

        def turn(block, carry):
            spot = pl.ds(pl.multiple_of(block * LANES, LANES), LANES)
            own = own_ref[:, spot].astype(jnp.float32)
            partner = partner_ref[:, spot].astype(jnp.float32)
            table_ref[spot, :] = jnp.concatenate([own, partner, blank], axis=0).T
            return carry

        lax.fori_loop(0, nodes // LANES, turn, 0, unroll=4)

    def body(group, carry):
        for step in range(UNROLL):
            target = group * UNROLL + step
            terms = [table_ref[pl.ds(ids_ref[k, target], 1), :] for k in range(fanout)]
            while len(terms) > 1:
                odd = terms[-1:] if len(terms) % 2 else []
                terms = [one + two for one, two in zip(terms[::2], terms[1::2])] + odd
            out_ref[pl.ds(target, 1), :] = terms[0]
        return carry

    lax.fori_loop(0, out_ref.shape[0] // UNROLL, body, 0)


def gather_sum(own, partner, ids):
    width, nodes = own.shape
    fanout, targets = ids.shape
    step_rows = min(512, targets)
    whole = pl.BlockSpec((width, nodes), lambda b: (0, 0), pipeline_mode=pl.Buffered(1))
    return pl.pallas_call(
        add_rows,
        grid=(targets // step_rows,),
        out_shape=jax.ShapeDtypeStruct((targets, LANES), jnp.float32),
        in_specs=[
            pl.BlockSpec((fanout, step_rows), lambda b: (0, b), memory_space=pltpu.SMEM),
            whole,
            whole,
        ],
        out_specs=pl.BlockSpec((step_rows, LANES), lambda b: (b, 0)),
        scratch_shapes=[pltpu.VMEM((nodes, LANES), jnp.float32)],
        compiler_params=pltpu.CompilerParams(
            vmem_limit_bytes=nodes * (LANES + width) * 4 + (8 << 20)
        ),
        cost_estimate=pl.CostEstimate(
            flops=targets * fanout * LANES,
            bytes_accessed=targets * fanout * LANES * 32,
            transcendentals=0,
        ),
        name="gather_sum",
    )(ids, own, partner)


def shards(
    node_features,
    neighbors_one,
    weight_self_one,
    weight_neigh_one,
    bias_one,
    weight_self_two,
    weight_neigh_two,
    send_rows,
    neighbors_two,
    degree_two,
    out_grad,
):
    devices = lax.axis_size("feat")
    hidden_width = weight_self_two.shape[0]
    own_seeds = out_grad.shape[0]
    targets = neighbors_one.shape[0]
    own_rows = targets // devices
    fanout_one = neighbors_one.shape[1]
    width = node_features.shape[0]
    pairs = devices // 2
    half = pairs * own_rows
    core = lax.axis_index("feat") % 2
    swap = [(d, d ^ 1) for d in range(devices)]
    same_core = [[2 * p + c for p in range(pairs)] for c in range(2)]

    def even_odd(own, other):
        first = jnp.where(core == 0, own, other)
        second = jnp.where(core == 0, other, own)
        return jnp.concatenate([first, second], axis=0)

    def to_blocks(columns):
        return lax.all_to_all(
            columns,
            "feat",
            split_axis=1,
            concat_axis=0,
            axis_index_groups=same_core,
            tiled=True,
        )

    def my_targets(columns):
        cut = columns.reshape(columns.shape[0], pairs, 2, own_rows)
        return lax.dynamic_index_in_dim(cut, core, 2, keepdims=False).reshape(-1, half)

    all_out_grad = lax.all_gather(out_grad, "feat", axis=0, tiled=True)
    spare = -width % 16
    features = jnp.pad(node_features, ((0, spare), (0, 0)))
    partner = lax.ppermute(features, "feat", swap)
    self_all = node_features[:, :targets]
    peer_rows = send_rows[0]
    slots_peer = peer_rows.shape[1]
    slot_total = devices * slots_peer
    fanout_two = neighbors_two.shape[1]
    keep_mask = jnp.arange(fanout_two, dtype=jnp.int32)[None, :] < degree_two[:, None]
    slot_ids = jnp.arange(slot_total, dtype=jnp.int32)
    slot_hits = (neighbors_two[:, :, None] == slot_ids[None, None, :]) & keep_mask[:, :, None]
    ref_count = jnp.sum(slot_hits.astype(jnp.float32), axis=1)
    degree_float = degree_two.astype(jnp.float32)[:, None]
    back_self = contract_last(out_grad, weight_self_two)
    per_neighbor = contract_last(out_grad, weight_neigh_two) / degree_float
    slot_grads = exact_lead(ref_count, per_neighbor)
    blocks = jnp.transpose(self_all.reshape(width, devices, own_rows), (1, 0, 2))
    slot_grads = slot_grads.astype(jnp.bfloat16).reshape(devices, -1, own_rows)
    swapped = lax.all_to_all(
        jnp.concatenate([blocks, slot_grads], axis=1),
        "feat",
        split_axis=0,
        concat_axis=0,
        tiled=True,
    )
    self_own = my_targets(self_all)
    self_other = my_targets(partner[:width, :targets])
    features, swapped = lax.optimization_barrier((features, swapped))
    self_cols = swapped[:, :width].reshape(devices * width, own_rows)
    returned = swapped[:, width:].reshape(slot_total, hidden_width)
    summed_one = gather_sum(features, partner, my_targets(neighbors_one.T))
    mean_pair = (summed_one[:, : 2 * (width + spare)] / fanout_one).astype(jnp.bfloat16).T
    mean_pair, all_out_grad = lax.optimization_barrier((mean_pair, all_out_grad))
    mean_own, mean_other = mean_pair[:width], mean_pair[width + spare :][:width]
    mean_cols = to_blocks(even_odd(mean_own, mean_other))
    pre_one = (
        contract_lead(self_cols, weight_self_one)
        + contract_lead(mean_cols, weight_neigh_one)
        + bias_one.astype(jnp.float32)
    )
    hidden_one = gelu_tanh(pre_one).astype(jnp.bfloat16)
    row_hits = (
        peer_rows.reshape(-1)[:, None] == jnp.arange(own_rows, dtype=jnp.int32)[None, :]
    ).astype(jnp.bfloat16)
    sent_rows = jnp.dot(row_hits, hidden_one, preferred_element_type=jnp.float32).astype(
        jnp.bfloat16
    )
    outgoing = sent_rows.reshape(devices, slots_peer, hidden_width)
    slot_out = exact_lead(ref_count / degree_float, out_grad.astype(jnp.float32))
    all_slot_out = lax.all_gather(slot_out.astype(jnp.bfloat16), "feat", axis=0, tiled=True)
    seed_hidden = hidden_one[:own_seeds]
    grad_hidden = contract_lead(row_hits, returned)
    grad_hidden = grad_hidden + jnp.pad(back_self, ((0, own_rows - own_seeds), (0, 0)))
    _, pull_back = jax.vjp(gelu_tanh, pre_one)
    grad_pre = pull_back(grad_hidden)[0].astype(jnp.bfloat16)
    order = list(range(0, pairs, 2)) + list(range(1, pairs, 2))[::-1]
    evens = (pairs + 1) // 2
    pair = lax.axis_index("feat") // 2
    mine = jnp.where(pair % 2 == 0, pair // 2, pairs - 1 - pair // 2)
    onward = [
        (2 * order[i] + c, 2 * order[(i + 1) % pairs] + c) for i in range(pairs) for c in range(2)
    ]
    back = [(there, here) for here, there in onward]
    left = jnp.concatenate([self_other, mean_other, self_own, mean_own], axis=0)
    left = jnp.transpose(left.reshape(4 * width, pairs, own_rows), (1, 0, 2))

    def term(hop, block):
        spot = lax.rem(mine + hop + pairs, pairs)
        owner = jnp.where(spot < evens, 2 * spot, 2 * (pairs - 1 - spot) + 1)
        return jnp.dot(
            lax.dynamic_index_in_dim(left, owner, 0, keepdims=False),
            block,
            preferred_element_type=jnp.float32,
        )

    side_rows = jnp.concatenate([seed_hidden, sent_rows], axis=0)
    side_rows = jnp.transpose(side_rows.reshape(own_seeds + slot_total, devices, -1), (1, 0, 2))
    outgoing = outgoing.reshape(devices, -1, side_rows.shape[2])
    side_rows = jnp.concatenate([side_rows, outgoing], axis=1)
    total = term(0, grad_pre)
    going, coming = grad_pre, grad_pre
    for hop in range(1, (pairs + 1) // 2):
        going = lax.ppermute(going, "feat", onward)
        coming = lax.ppermute(coming, "feat", back)
        if hop == 1:
            side_rows, going, coming = lax.optimization_barrier((side_rows, going, coming))
        total = total + term(-hop, going) + term(hop, coming)
    if pairs % 2 == 0:
        cut = own_rows // 2
        first = lax.ppermute(going[:cut], "feat", onward)
        second = lax.ppermute(coming[cut:], "feat", back)
        total = total + term(pairs // 2, jnp.concatenate([first, second], axis=0))
    from_other = lax.ppermute(total[: 2 * width], "feat", swap)
    both_one = total[2 * width :] + from_other

    side_rows = lax.all_to_all(side_rows, "feat", split_axis=0, concat_axis=0, tiled=True)
    incoming = side_rows[:, own_seeds + slot_total :]
    summed_two = jnp.dot(
        ref_count.astype(jnp.bfloat16),
        incoming.reshape(slot_total, hidden_width),
        preferred_element_type=jnp.float32,
    )
    mean_two = (summed_two / degree_float).astype(jnp.bfloat16)
    out_full = jnp.dot(seed_hidden, weight_self_two, preferred_element_type=jnp.float32) + jnp.dot(
        mean_two, weight_neigh_two, preferred_element_type=jnp.float32
    )
    layer_out = out_full.astype(jnp.bfloat16)

    slice_two = side_rows.shape[2]
    seed_cols = side_rows[:, :own_seeds].reshape(-1, slice_two)
    sent_cols = side_rows[:, own_seeds : own_seeds + slot_total].reshape(devices, devices, slots_peer, slice_two)
    sent_cols = jnp.transpose(sent_cols, (1, 0, 2, 3)).reshape(-1, slice_two)
    return (
        layer_out,
        both_one[:width],
        both_one[width:],
        contract_lead(seed_cols, all_out_grad),
        contract_lead(sent_cols, all_slot_out),
    )


def solution(mesh):
    return jax.shard_map(
        shards,
        mesh=mesh,
        in_specs=(
            P("feat", "groups"),
            P("groups", None),
            P(),
            P(),
            P(),
            P(),
            P(),
            P("feat", None, "groups"),
            P(("groups", "feat"), None),
            P(("groups", "feat")),
            P(("groups", "feat"), None),
        ),
        out_specs=(
            P(("groups", "feat"), None),
            P("feat", "groups"),
            P("feat", "groups"),
            P("feat", "groups"),
            P("feat", "groups"),
        ),
        check_vma=False,
    )
```
